32 devices in a mesh: ctx: 16 (over z, y, x), ch: 2 (over core).
Axes of the slice: x: 2, y: 2, z: 4, core: 2. Of those that a mesh axis runs over, the one named last changes fastest.
Arguments:
- first_gate: bfloat16 [2048, 8192], P('ctx', 'ch'), may hold values from -6 to 6
- second_gate: bfloat16 [2048, 8192], P('ctx', 'ch'), may hold values from -6 to 6
- output_gate: bfloat16 [2048, 8192], P('ctx', 'ch'), may hold values from -6 to 6
- values: bfloat16 [2048, 8192], P('ctx', 'ch'), may hold values from -6 to 6
- cotangent: bfloat16 [2048, 8192], P('ctx', 'ch'), may hold values from -6 to 6
- medium_filter: bfloat16 [128, 512], P(None, 'ch'), may hold values from -0.5 to 0.5
- long_filter: bfloat16 [2048, 512], P('ctx', 'ch'), may hold values from -0.088388348 to 0.088388348
Outputs:
- grad_first: bfloat16 [2048, 8192], P('ctx', 'ch')
- grad_second: bfloat16 [2048, 8192], P('ctx', 'ch')
- grad_output_gate: bfloat16 [2048, 8192], P('ctx', 'ch')
- grad_values: bfloat16 [2048, 8192], P('ctx', 'ch')
- grad_medium: float32 [128, 512], P(None, 'ch')
- grad_long: bfloat16 [2048, 512], P('ctx', 'ch')
- filter_rms: float32 [], replicated
The draws below stay inside these ranges and needn't reach their ends.
All inputs are finite; a program needn't handle non-finite values.
Results may differ from the reference program's by a relative error of at most 0.011.
Values may be sent and summed in bfloat16 or wider, within the bound.
A program may use at most 128 MiB of HBM per device.

```python
import math
import jax
import jax.numpy as jnp
from jax import lax

D = 8192
TAPS = 128
GROUP = 16
TOKENS = 2048
GROUPS = 512
N_CH = 2


def draw_long_filter(key, part):
    noise_key, rate_key = jax.random.split(jax.random.fold_in(key, 17))
    group_count = D // GROUP
    positions = jnp.arange(TOKENS, dtype=jnp.float32)[:, None]
    noise = jnp.clip(jax.random.normal(noise_key, (TOKENS, group_count), jnp.float32), -4.0, 4.0)
    rates = jnp.exp(jax.random.uniform(rate_key, (1, group_count), jnp.float32, math.log(0.5), math.log(40.0)))
    filt = noise * jnp.exp(-rates * positions / TOKENS) / math.sqrt(TOKENS)
    return filt.astype(jnp.bfloat16)


def block_scale(stream_key, extent, cuts, least, top_value):
    def one(position, shards_of):
        steps = jax.random.uniform(jax.random.fold_in(jax.random.fold_in(stream_key, 6), position), (shards_of,), jnp.float32, least / len(cuts), top_value / len(cuts))
        return jnp.repeat(jnp.exp(steps), extent[position] // shards_of).reshape((-1,) + (1,) * (len(extent) - position - 1))

    level = one(*cuts[0])
    for cut in cuts[1:]:
        level = level * one(*cut)
    return level


def bell_draw(key, extent, width, reach, shards=(), kind=jnp.bfloat16):
    drawn = jax.random.normal(key, extent, jnp.float32) * width
    if len(shards) > 0:
        drawn = block_scale(key, extent, shards, -0.22, 0.18) * drawn
    return jnp.clip(drawn, min=-reach, max=reach).astype(kind)


def setup_inputs(seed: int = 0) -> dict:
    keys = jax.random.split(jax.random.key(seed), 8)
    first_gate = bell_draw(keys[0], (TOKENS, D), 1.0, 6.0, ((0, 16), (1, 2)))
    second_gate = bell_draw(keys[1], (TOKENS, D), 1.0, 6.0, ((0, 16), (1, 2)))
    output_gate = bell_draw(keys[2], (TOKENS, D), 1.0, 6.0, ((0, 16), (1, 2)))
    values = bell_draw(keys[3], (TOKENS, D), 1.0, 6.0, ((0, 16), (1, 2)))
    cotangent = bell_draw(keys[4], (TOKENS, D), 1.0, 6.0, ((0, 16), (1, 2)))
    medium_filter = bell_draw(keys[5], (TAPS, GROUPS), TAPS ** -0.5, 0.5, ((1, 2),))
    long_filter = draw_long_filter(jax.random.fold_in(keys[7], 71), 0)
    return {"first_gate": first_gate, "second_gate": second_gate, "output_gate": output_gate, "values": values, "cotangent": cotangent, "medium_filter": medium_filter, "long_filter": long_filter}


def rounded(value):
    return lax.optimization_barrier(value.astype(jnp.bfloat16)).astype(jnp.float32)

def reference(first_gate, second_gate, output_gate, values, cotangent, medium_filter, long_filter):
    seq_len, model_width = first_gate.shape
    tap_count, group_total = medium_filter.shape
    group_size = model_width // group_total
    block_total = N_CH
    block_width = model_width // block_total
    block_groups = group_total // block_total
    scale = 1.0 / math.sqrt(seq_len * group_size)
    fft_len = 2 * seq_len

    def by_block(matrix):
        return matrix.reshape(matrix.shape[0], block_total, -1).transpose(1, 0, 2)

    def unblock(stacked):
        return stacked.transpose(1, 0, 2).reshape(stacked.shape[1], -1)

    def one_block(operands):
        gate_one, gate_two, gate_three, value_part, grad_part, medium_part, long_part = operands
        gate_one = gate_one.astype(jnp.float32)
        gate_two = gate_two.astype(jnp.float32)
        gate_three = gate_three.astype(jnp.float32)
        value_part = value_part.astype(jnp.float32)
        grad_part = grad_part.astype(jnp.float32)
        medium_wide = jnp.repeat(medium_part.astype(jnp.float32), group_size, axis=1)
        gated = rounded(gate_one * value_part)
        padded_gate = jnp.concatenate([jnp.zeros((tap_count - 1, block_width), jnp.float32), gated], axis=0)

        def forward_tap(tap, total):
            start = (tap_count - 1 - tap).astype(jnp.int32)
            return total + medium_wide[tap] * lax.dynamic_slice_in_dim(padded_gate, start, seq_len, 0)
        mixed = lax.fori_loop(0, tap_count, forward_tap, jnp.zeros((seq_len, block_width), jnp.float32))
        carried = rounded(gate_two * mixed)
        inner = rounded(grad_part * gate_three)
        long_spec = jnp.fft.rfft(long_part.astype(jnp.float32), n=fft_len, axis=0)
        long_wide = jnp.repeat(long_spec, group_size, axis=1)
        carried_spec = jnp.fft.rfft(carried, n=fft_len, axis=0)
        inner_spec = jnp.fft.rfft(inner, n=fft_len, axis=0)
        second = rounded(jnp.fft.irfft(carried_spec * long_wide, n=fft_len, axis=0)[:seq_len])
        grad_carried = rounded(jnp.fft.irfft(inner_spec * jnp.conj(long_wide), n=fft_len, axis=0)[:seq_len])
        corr_spec = (inner_spec * jnp.conj(carried_spec)).reshape(-1, block_groups, group_size).sum(axis=2)
        grad_long = (jnp.fft.irfft(corr_spec, n=fft_len, axis=0)[:seq_len] * scale).astype(jnp.bfloat16)
        grad_output_gate = (grad_part * second).astype(jnp.bfloat16)
        grad_second = (grad_carried * mixed).astype(jnp.bfloat16)
        grad_mixed = rounded(grad_carried * gate_two)
        trailing = jnp.concatenate([grad_mixed, jnp.zeros((tap_count - 1, block_width), jnp.float32)], axis=0)

        def backward_tap(tap, total):
            start = jnp.asarray(tap).astype(jnp.int32)
            return total + medium_wide[tap] * lax.dynamic_slice_in_dim(trailing, start, seq_len, 0)
        grad_gated = lax.fori_loop(0, tap_count, backward_tap, jnp.zeros((seq_len, block_width), jnp.float32))
        grad_first = (grad_gated * value_part).astype(jnp.bfloat16)
        grad_values = (grad_gated * gate_one).astype(jnp.bfloat16)

        def medium_lag(tap):
            start = (tap_count - 1 - tap).astype(jnp.int32)
            shifted = lax.dynamic_slice_in_dim(padded_gate, start, seq_len, 0)
            return lax.optimization_barrier(jnp.sum((grad_mixed * shifted).reshape(seq_len, block_groups, group_size), axis=(0, 2))) * scale
        grad_medium = lax.map(medium_lag, jnp.arange(tap_count, dtype=jnp.int32))
        return (grad_first, grad_second, grad_output_gate, grad_values, grad_medium, grad_long)
    stacked = (by_block(first_gate), by_block(second_gate), by_block(output_gate), by_block(values), by_block(cotangent), by_block(medium_filter), by_block(long_filter))
    results = lax.map(one_block, stacked)
    grad_first = unblock(results[0])
    grad_second = unblock(results[1])
    grad_output_gate = unblock(results[2])
    grad_values = unblock(results[3])
    grad_medium = unblock(results[4])
    grad_long = unblock(results[5])
    squares = jnp.sum(jnp.square(grad_long.astype(jnp.float32))) + jnp.sum(jnp.square(grad_medium))
    filter_rms = jnp.sqrt(squares / ((seq_len + tap_count) * group_total))
    return (grad_first, grad_second, grad_output_gate, grad_values, grad_medium, grad_long, filter_rms)
```

```python
import functools
import math

import jax
import jax.numpy as jnp
from jax import lax
from jax.experimental import pallas as pl
from jax.experimental.pallas import tpu as pltpu
from jax.sharding import PartitionSpec as P

wide = jnp.float32
narrow = jnp.bfloat16
params = pltpu.CompilerParams(vmem_limit_bytes=48 * 1024 * 1024)


def rolled_rows(row, rows):
    width = row.shape[1]
    base = pltpu.roll(jnp.broadcast_to(row, (16, width)), 0, 1, stride=1, stride_axis=0)
    parts = [base]
    for number in range(1, rows // 16):
        parts.append(pltpu.roll(base, 16 * number, 1))
    return jnp.concatenate([part.astype(narrow) for part in parts], axis=0)


def diagonal_sums(table):
    rows, width = table.shape
    while rows > 8:
        rows = rows // 2
        table = table[:rows] + pltpu.roll(table[rows:], width - rows, 1)
    total = table[0:1]
    for number in range(1, rows):
        total = total + pltpu.roll(table[number : number + 1], width - number, 1)
    return total


def prep_kernel(first_ref, values_ref, cotangent_ref, output_ref, gated_ref, inner_ref):
    gated = first_ref[...].astype(wide) * values_ref[...].astype(wide)
    gated_ref[...] = gated.astype(narrow).T
    inner = cotangent_ref[...].astype(wide) * output_ref[...].astype(wide)
    inner_ref[...] = inner.astype(narrow).T


def forward_kernel(size, base_ref, prior_ref, gated_ref, second_ref, mixed_ref, carried_ref):
    gate = second_ref[...].T
    for number in range(base_ref.shape[0]):
        rows = slice(number * size, (number + 1) * size)
        extended = jnp.concatenate([prior_ref[rows], gated_ref[rows]], axis=1)
        band = rolled_rows(base_ref[number : number + 1, :], gated_ref.shape[1])
        mixed = lax.dot_general(
            extended, band, (((1,), (1,)), ((), ())), preferred_element_type=wide
        )
        mixed_ref[rows] = mixed
        carried_ref[rows] = (gate[rows].astype(wide) * mixed).astype(narrow)


def filter_table(row, block):
    table = rolled_rows(row, block)
    lanes = lax.broadcasted_iota(jnp.int32, (block, block), 1)
    rows = lax.broadcasted_iota(jnp.int32, (block, block), 0)
    head = jnp.where(lanes >= rows, table[:, :block].astype(wide), 0.0).astype(narrow)
    return head, table


def back_kernel(filter_ref, inner_ref, out_ref, table_ref, pair_ref, total_ref):
    blocks, size, block = inner_ref.shape
    count = blocks * size
    head, table = filter_table(filter_ref[0], block)
    table_ref[...] = table
    table_ref[:, :block] = head
    inner = inner_ref[...].reshape(count, block)
    pair_ref[:, :block] = inner
    pair_ref[: count - size, block:] = inner[size:]
    pair_ref[count - size :, block:] = jnp.zeros((size, block), narrow)
    for lag in range(0, blocks, 2):
        rows = count - lag * size
        product = lax.dot_general(
            pair_ref[lag * size :, :],
            table_ref[:, lag * block : (lag + 2) * block],
            (((1,), (1,)), ((), ())),
            preferred_element_type=wide,
        )
        if lag == 0:
            total_ref[...] = product
        else:
            total_ref[:rows] += product
    out_ref[...] = total_ref[...].astype(narrow).reshape(blocks, size, block)


def ahead_kernel(
    scale,
    filter_ref,
    carried_ref,
    inner_ref,
    out_ref,
    long_ref,
    table_ref,
    pair_ref,
    total_ref,
    padded_ref,
    lagged_ref,
):
    blocks, size, block = inner_ref.shape
    count = blocks * size
    head, table = filter_table(filter_ref[0], block)
    table_ref[...] = table
    table_ref[:, :block] = head
    carried = carried_ref[...].reshape(count, block)
    pair_ref[:, :block] = carried
    pair_ref[size:, block:] = carried[: count - size]
    pair_ref[:size, block:] = jnp.zeros((size, block), narrow)
    padded_ref[:count] = inner_ref[...].reshape(count, block)
    padded_ref[count:] = jnp.zeros((count, block), narrow)
    for lag in range(0, blocks, 2):
        rows = count - lag * size
        weights = jnp.concatenate(
            [
                table_ref[:, lag * block : (lag + 1) * block],
                table_ref[:, (lag + 1) * block : (lag + 2) * block],
            ],
            axis=0,
        )
        product = jnp.dot(pair_ref[:rows, :], weights, preferred_element_type=wide)
        if lag == 0:
            total_ref[...] = product
        else:
            total_ref[lag * size :] += product
    out_ref[...] = total_ref[...].astype(narrow).reshape(blocks, size, block)
    turned = carried.T
    for lag in range(0, blocks, 2):
        weights = jnp.concatenate(
            [
                padded_ref[lag * size : lag * size + count],
                padded_ref[(lag + 1) * size : (lag + 1) * size + count],
            ],
            axis=1,
        )
        lagged_ref[:, lag * block : (lag + 2) * block] = jnp.dot(
            turned, weights, preferred_element_type=wide
        )
    lanes = lax.broadcasted_iota(jnp.int32, (block, block), 1)
    rows = lax.broadcasted_iota(jnp.int32, (block, block), 0)
    lagged_ref[:, :block] = jnp.where(lanes >= rows, lagged_ref[:, :block], 0.0)
    long_ref[0] = (diagonal_sums(lagged_ref[...]) * scale).astype(narrow)


def mixed_grad_kernel(
    size, back_ref, second_ref, mixed_ref, gated_ref, prior_ref, grad_second_ref, grad_mixed_ref, sums_ref
):
    tokens = second_ref.shape[0]
    back = back_ref[...].astype(wide)
    grad_second_ref[...] = (back * mixed_ref[...]).T.astype(narrow)
    grad_mixed = (back_ref[...].T.astype(wide) * second_ref[...].astype(wide)).astype(narrow)
    grad_mixed_ref[...] = grad_mixed.T
    per = 128 // size
    for number in range(sums_ref.shape[0]):
        rows = slice(number * size, (number + 1) * size)
        extended = jnp.concatenate([prior_ref[rows], gated_ref[rows]], axis=1)
        place = number % per
        pieces = []
        if place > 0:
            pieces.append(jnp.zeros((place * size, 2 * tokens), narrow))
        pieces.append(extended)
        if place < per - 1:
            pieces.append(jnp.zeros(((per - 1 - place) * size, 2 * tokens), narrow))
        weights = jnp.concatenate(pieces, axis=0)
        start = number // per * 128
        product = jnp.dot(
            grad_mixed[:, start : start + 128], weights, preferred_element_type=wide
        )
        sums_ref[number : number + 1, :] = diagonal_sums(product)


def gate_grad_kernel(
    size, base_ref, grad_mixed_ref, after_ref, first_ref, values_ref, grad_first_ref, grad_values_ref, total_ref
):
    for number in range(base_ref.shape[0]):
        rows = slice(number * size, (number + 1) * size)
        extended = jnp.concatenate([grad_mixed_ref[rows], after_ref[rows]], axis=1)
        band = rolled_rows(base_ref[number : number + 1, :], grad_mixed_ref.shape[1])
        total_ref[rows] = lax.dot_general(
            extended, band, (((1,), (1,)), ((), ())), preferred_element_type=wide
        )
    grad_gated = total_ref[...].T
    grad_first_ref[...] = (grad_gated * values_ref[...].astype(wide)).astype(narrow)
    grad_values_ref[...] = (grad_gated * first_ref[...].astype(wide)).astype(narrow)


def output_grad_kernel(ahead_ref, cotangent_ref, grad_output_ref):
    ahead = ahead_ref[...].T.astype(wide)
    grad_output_ref[...] = (cotangent_ref[...].astype(wide) * ahead).astype(narrow)


def shape_of(shape, kind):
    return jax.ShapeDtypeStruct(shape, kind)


def body(first_gate, second_gate, output_gate, values, cotangent, medium_filter, long_filter):
    tokens, channels = first_gate.shape
    taps, groups = medium_filter.shape
    size = channels // groups
    ctx = lax.axis_size("ctx")
    own = groups // ctx
    step_groups = math.gcd(groups, 16)
    width = step_groups * size
    steps = (groups // step_groups,)

    by_token = pl.BlockSpec((tokens, width), lambda i: (0, i))
    by_channel = pl.BlockSpec((width, tokens), lambda i: (i, 0))
    base_block = pl.BlockSpec((step_groups, 2 * tokens), lambda i: (i, 0))
    channel_shape = (channels, tokens)

    gated, inner = pl.pallas_call(
        prep_kernel,
        grid=steps,
        in_specs=[by_token] * 4,
        out_specs=[by_channel] * 2,
        out_shape=[shape_of(channel_shape, narrow)] * 2,
        compiler_params=params,
    )(first_gate, values, cotangent, output_gate)

    def swapped(array):
        return lax.all_to_all(array, "ctx", split_axis=0, concat_axis=0, tiled=True)

    filters = swapped(long_filter.T.reshape(ctx, own, tokens))
    inner_all = swapped(inner.reshape(ctx, own * size, tokens))
    prior = lax.ppermute(gated, "ctx", [(i, i + 1) for i in range(ctx - 1)])

    turned = medium_filter.T.astype(wide)
    pad = 2 * tokens - taps
    forward_base = jnp.concatenate(
        [
            jnp.zeros((groups, tokens + 1 - taps), wide),
            turned[:, ::-1],
            jnp.zeros((groups, tokens - 1), wide),
        ],
        axis=1,
    )
    reverse_base = jnp.concatenate([turned, jnp.zeros((groups, pad), wide)], axis=1)

    mixed, carried = pl.pallas_call(
        functools.partial(forward_kernel, size),
        grid=steps,
        in_specs=[base_block, by_channel, by_channel, by_token],
        out_specs=[by_channel] * 2,
        out_shape=[shape_of(channel_shape, wide), shape_of(channel_shape, narrow)],
        compiler_params=params,
    )(forward_base, prior, gated, second_gate)
    carried_all = swapped(carried.reshape(ctx, own * size, tokens))

    length = ctx * tokens
    filter_rows = filters.transpose(1, 0, 2).reshape(own, 1, length).astype(wide)
    row_block = pl.BlockSpec((1, 1, length), lambda g: (g, 0, 0))
    piece = pl.BlockSpec((ctx, size, tokens), lambda g: (0, g, 0))
    all_shape = (ctx, own * size, tokens)
    scratch = [
        pltpu.VMEM((tokens, length), narrow),
        pltpu.VMEM((ctx * size, 2 * tokens), narrow),
        pltpu.VMEM((ctx * size, tokens), wide),
    ]
    back_all = pl.pallas_call(
        back_kernel,
        grid=(own,),
        in_specs=[row_block, piece],
        out_specs=piece,
        out_shape=shape_of(all_shape, narrow),
        scratch_shapes=scratch,
        compiler_params=params,
    )(filter_rows, inner_all)
    back = swapped(back_all).reshape(channel_shape)

    scale = 1.0 / math.sqrt(length * size)
    ahead_all, long_rows = pl.pallas_call(
        functools.partial(ahead_kernel, scale),
        grid=(own,),
        in_specs=[row_block, piece, piece],
        out_specs=[piece, row_block],
        out_shape=[shape_of(all_shape, narrow), shape_of((own, 1, length), narrow)],
        scratch_shapes=scratch
        + [
            pltpu.VMEM((2 * ctx * size, tokens), narrow),
            pltpu.VMEM((tokens, length), wide),
        ],
        compiler_params=params,
    )(filter_rows, carried_all, inner_all)
    ahead = swapped(ahead_all).reshape(channel_shape)
    long_pieces = long_rows.reshape(own, ctx, tokens).transpose(1, 0, 2)
    grad_long = swapped(long_pieces).reshape(groups, tokens).T

    grad_second, grad_mixed, sums = pl.pallas_call(
        functools.partial(mixed_grad_kernel, size),
        grid=steps,
        in_specs=[by_channel, by_token, by_channel, by_channel, by_channel],
        out_specs=[by_token, by_channel, base_block],
        out_shape=[
            shape_of((tokens, channels), narrow),
            shape_of(channel_shape, narrow),
            shape_of((groups, 2 * tokens), wide),
        ],
        compiler_params=params,
    )(back, second_gate, mixed, gated, prior)
    after = lax.ppermute(grad_mixed, "ctx", [(i + 1, i) for i in range(ctx - 1)])

    terms = sums[:, tokens + 1 - taps : tokens + 1][:, ::-1] * scale
    medium_own = jnp.sum(swapped(terms.reshape(ctx, own, taps)), axis=0)
    squares = jnp.sum(jnp.square(medium_own)) + jnp.sum(jnp.square(long_rows.astype(wide)))
    package = jnp.concatenate([medium_own, jnp.full((1, taps), squares, wide)], axis=0)
    gathered = swapped(jnp.broadcast_to(package[None], (ctx, own + 1, taps)))
    grad_medium = gathered[:, :own].reshape(groups, taps).T
    ch = lax.axis_size("ch")
    side = jnp.broadcast_to(jnp.sum(gathered[:, own], axis=0)[None, None], (ch, 1, taps))
    total = jnp.sum(
        lax.all_to_all(side, "ch", split_axis=0, concat_axis=0, tiled=True), axis=0
    )[0, 0]
    filter_rms = jnp.sqrt(total / ((length + taps) * groups * ch))

    grad_first, grad_values = pl.pallas_call(
        functools.partial(gate_grad_kernel, size),
        grid=steps,
        in_specs=[base_block, by_channel, by_channel, by_token, by_token],
        out_specs=[by_token] * 2,
        out_shape=[shape_of((tokens, channels), narrow)] * 2,
        scratch_shapes=[pltpu.VMEM((width, tokens), wide)],
        compiler_params=params,
    )(reverse_base, grad_mixed, after, first_gate, values)
    grad_output_gate = pl.pallas_call(
        output_grad_kernel,
        grid=steps,
        in_specs=[by_channel, by_token],
        out_specs=by_token,
        out_shape=shape_of((tokens, channels), narrow),
        compiler_params=params,
    )(ahead, cotangent)
    return (
        grad_first,
        grad_second,
        grad_output_gate,
        grad_values,
        grad_medium,
        grad_long,
        filter_rms,
    )


def solution(mesh):
    spread = P("ctx", "ch")
    shared = P(None, "ch")
    return jax.shard_map(
        body,
        mesh=mesh,
        in_specs=(spread, spread, spread, spread, spread, shared, spread),
        out_specs=(spread, spread, spread, spread, shared, spread, P()),
        check_vma=False,
    )
```

```python
import functools
import math

import jax
import jax.numpy as jnp
from jax import lax
from jax.experimental import pallas as pl
from jax.experimental.pallas import tpu as pltpu
from jax.sharding import PartitionSpec as P

wide = jnp.float32
narrow = jnp.bfloat16
params = pltpu.CompilerParams(vmem_limit_bytes=48 * 1024 * 1024)
peak = 1.1e9


def cost(micros, channels):
    scaled = int(micros * peak * channels / 4096)
    return pl.CostEstimate(flops=scaled, bytes_accessed=0, transcendentals=0)


def rolled_rows(row, rows):
    width = row.shape[1]
    base = pltpu.roll(jnp.broadcast_to(row, (16, width)), 0, 1, stride=1, stride_axis=0)
    base = base.astype(narrow)
    parts = [base]
    for number in range(1, rows // 16):
        parts.append(pltpu.roll(base, 16 * number, 1))
    return jnp.concatenate([part.astype(narrow) for part in parts], axis=0)


def diagonal_sums(table):
    rows, width = table.shape
    while rows > 8:
        rows = rows // 2
        table = table[:rows] + pltpu.roll(table[rows:], width - rows, 1)
    total = table[0:1]
    for number in range(1, rows):
        total = total + pltpu.roll(table[number : number + 1], width - number, 1)
    return total


def gated_kernel(first_ref, values_ref, gated_ref):
    gated = first_ref[...].astype(wide) * values_ref[...].astype(wide)
    gated_ref[...] = gated.astype(narrow).T


def inner_kernel(cotangent_ref, output_ref, filter_ref, slab_ref):
    inner = cotangent_ref[...].astype(wide) * output_ref[...].astype(wide)
    width = inner.shape[1]
    slab_ref[0, :width] = inner.astype(narrow).T
    slab_ref[0, width:] = filter_ref[0]


def forward_kernel(size, base_ref, prior_ref, gated_ref, second_ref, mixed_ref, carried_ref):
    gate = second_ref[...].T
    for number in range(base_ref.shape[0]):
        rows = slice(number * size, (number + 1) * size)
        extended = jnp.concatenate([prior_ref[rows], gated_ref[rows]], axis=1)
        band = rolled_rows(base_ref[number : number + 1, :], gated_ref.shape[1])
        mixed = lax.dot_general(
            extended, band, (((1,), (1,)), ((), ())), preferred_element_type=wide
        )
        mixed_ref[rows] = mixed
        carried_ref[rows] = (gate[rows].astype(wide) * mixed).astype(narrow)


def filter_table(row, block):
    table = rolled_rows(row, block)
    lanes = lax.broadcasted_iota(jnp.int32, (block, block), 1)
    rows = lax.broadcasted_iota(jnp.int32, (block, block), 0)
    head = jnp.where(lanes >= rows, table[:, :block].astype(wide), 0.0).astype(narrow)
    return head, table


def back_kernel(filter_ref, inner_ref, out_ref, table_ref, pair_ref, total_ref):
    blocks, size, block = inner_ref.shape
    count = blocks * size
    head, table = filter_table(filter_ref[0], block)
    table_ref[...] = table
    table_ref[:, :block] = head
    inner = inner_ref[...].reshape(count, block)
    pair_ref[:, :block] = inner
    pair_ref[: count - size, block:] = inner[size:]
    pair_ref[count - size :, block:] = jnp.zeros((size, block), narrow)
    for lag in range(0, blocks, 2):
        rows = count - lag * size
        product = lax.dot_general(
            pair_ref[lag * size :, :],
            table_ref[:, lag * block : (lag + 2) * block],
            (((1,), (1,)), ((), ())),
            preferred_element_type=wide,
        )
        if lag == 0:
            total_ref[...] = product
        else:
            total_ref[:rows] += product
    out_ref[...] = total_ref[...].astype(narrow).reshape(blocks, size, block)


def ahead_kernel(
    scale,
    filter_ref,
    carried_ref,
    inner_ref,
    out_ref,
    long_ref,
    table_ref,
    pair_ref,
    total_ref,
    padded_ref,
    lagged_ref,
):
    blocks, size, block = inner_ref.shape
    count = blocks * size
    head, table = filter_table(filter_ref[0], block)
    table_ref[...] = table
    table_ref[:, :block] = head
    carried = carried_ref[...].reshape(count, block)
    pair_ref[:, :block] = carried
    pair_ref[size:, block:] = carried[: count - size]
    pair_ref[:size, block:] = jnp.zeros((size, block), narrow)
    padded_ref[:count] = inner_ref[...].reshape(count, block)
    padded_ref[count:] = jnp.zeros((count, block), narrow)
    for lag in range(0, blocks, 2):
        rows = count - lag * size
        weights = jnp.concatenate(
            [
                table_ref[:, lag * block : (lag + 1) * block],
                table_ref[:, (lag + 1) * block : (lag + 2) * block],
            ],
            axis=0,
        )
        product = jnp.dot(pair_ref[:rows, :], weights, preferred_element_type=wide)
        if lag == 0:
            total_ref[...] = product
        else:
            total_ref[lag * size :] += product
    out_ref[...] = total_ref[...].astype(narrow).reshape(blocks, size, block)
    turned = carried.T
    for lag in range(0, blocks, 2):
        weights = jnp.concatenate(
            [
                padded_ref[lag * size : lag * size + count],
                padded_ref[(lag + 1) * size : (lag + 1) * size + count],
            ],
            axis=1,
        )
        lagged_ref[:, lag * block : (lag + 2) * block] = jnp.dot(
            turned, weights, preferred_element_type=wide
        )
    lanes = lax.broadcasted_iota(jnp.int32, (block, block), 1)
    rows = lax.broadcasted_iota(jnp.int32, (block, block), 0)
    lagged_ref[:, :block] = jnp.where(lanes >= rows, lagged_ref[:, :block], 0.0)
    long_ref[0] = (diagonal_sums(lagged_ref[...]) * scale).astype(narrow)


def mixed_grad_kernel(
    size, back_ref, second_ref, mixed_ref, gated_ref, prior_ref, grad_second_ref, grad_mixed_ref, sums_ref
):
    tokens = second_ref.shape[0]
    back = back_ref[...].astype(wide)
    grad_second_ref[...] = (back * mixed_ref[...]).T.astype(narrow)
    grad_mixed = (back_ref[...].T.astype(wide) * second_ref[...].astype(wide)).astype(narrow)
    grad_mixed_ref[...] = grad_mixed.T
    per = 128 // size
    for number in range(sums_ref.shape[0]):
        rows = slice(number * size, (number + 1) * size)
        extended = jnp.concatenate([prior_ref[rows], gated_ref[rows]], axis=1)
        place = number % per
        pieces = []
        if place > 0:
            pieces.append(jnp.zeros((place * size, 2 * tokens), narrow))
        pieces.append(extended)
        if place < per - 1:
            pieces.append(jnp.zeros(((per - 1 - place) * size, 2 * tokens), narrow))
        weights = jnp.concatenate(pieces, axis=0)
        start = number // per * 128
        product = jnp.dot(
            grad_mixed[:, start : start + 128], weights, preferred_element_type=wide
        )
        sums_ref[number : number + 1, :] = diagonal_sums(product)


def gate_grad_kernel(
    size, base_ref, grad_mixed_ref, after_ref, first_ref, values_ref, grad_first_ref, grad_values_ref, total_ref
):
    for number in range(base_ref.shape[0]):
        rows = slice(number * size, (number + 1) * size)
        extended = jnp.concatenate([grad_mixed_ref[rows], after_ref[rows]], axis=1)
        band = rolled_rows(base_ref[number : number + 1, :], grad_mixed_ref.shape[1])
        total_ref[rows] = lax.dot_general(
            extended, band, (((1,), (1,)), ((), ())), preferred_element_type=wide
        )
    grad_gated = total_ref[...].T
    grad_first_ref[...] = (grad_gated * values_ref[...].astype(wide)).astype(narrow)
    grad_values_ref[...] = (grad_gated * first_ref[...].astype(wide)).astype(narrow)


def output_grad_kernel(ahead_ref, cotangent_ref, grad_output_ref):
    ahead = ahead_ref[...].T.astype(wide)
    grad_output_ref[...] = (cotangent_ref[...].astype(wide) * ahead).astype(narrow)


def shape_of(shape, kind):
    return jax.ShapeDtypeStruct(shape, kind)


def body(first_gate, second_gate, output_gate, values, cotangent, medium_filter, long_filter):
    tokens, channels = first_gate.shape
    taps, groups = medium_filter.shape
    size = channels // groups
    ctx = lax.axis_size("ctx")
    own = groups // ctx
    step_groups = math.gcd(groups, 16)
    width = step_groups * size
    steps = (groups // step_groups,)

    by_token = pl.BlockSpec((tokens, width), lambda i: (0, i))
    by_channel = pl.BlockSpec((width, tokens), lambda i: (i, 0))
    base_block = pl.BlockSpec((step_groups, 2 * tokens), lambda i: (i, 0))
    channel_shape = (channels, tokens)

    gated = pl.pallas_call(
        gated_kernel,
        grid=steps,
        in_specs=[by_token] * 2,
        out_specs=by_channel,
        out_shape=shape_of(channel_shape, narrow),
        compiler_params=params,
        cost_estimate=cost(5, channels),
    )(first_gate, values)
    prior = lax.ppermute(gated, "ctx", [(i, i + 1) for i in range(ctx - 1)])

    def swapped(array):
        return lax.all_to_all(array, "ctx", split_axis=0, concat_axis=0, tiled=True)

    slab_width = own * size
    slab_token = pl.BlockSpec((tokens, slab_width), lambda i: (0, i))
    if slab_width % 128:
        slab = jnp.concatenate(
            [
                (cotangent.astype(wide) * output_gate.astype(wide))
                .astype(narrow)
                .T.reshape(ctx, slab_width, tokens),
                long_filter.T.reshape(ctx, own, tokens),
            ],
            axis=1,
        )
    else:
        slab = pl.pallas_call(
            inner_kernel,
            grid=(ctx,),
            in_specs=[
                slab_token,
                slab_token,
                pl.BlockSpec((1, own, tokens), lambda i: (i, 0, 0)),
            ],
            out_specs=pl.BlockSpec((1, slab_width + own, tokens), lambda i: (i, 0, 0)),
            out_shape=shape_of((ctx, slab_width + own, tokens), narrow),
            compiler_params=params,
            cost_estimate=cost(5, channels),
        )(cotangent, output_gate, long_filter.T.reshape(ctx, own, tokens))
    slab, prior = lax.optimization_barrier((slab, prior))
    slab_all = swapped(slab)

    turned = medium_filter.T.astype(wide)
    pad = 2 * tokens - taps
    forward_base = jnp.concatenate(
        [
            jnp.zeros((groups, tokens + 1 - taps), wide),
            turned[:, ::-1],
            jnp.zeros((groups, tokens - 1), wide),
        ],
        axis=1,
    )
    reverse_base = jnp.concatenate([turned, jnp.zeros((groups, pad), wide)], axis=1)

    mixed, carried = pl.pallas_call(
        functools.partial(forward_kernel, size),
        grid=steps,
        in_specs=[base_block, by_channel, by_channel, by_token],
        out_specs=[by_channel] * 2,
        out_shape=[shape_of(channel_shape, wide), shape_of(channel_shape, narrow)],
        compiler_params=params,
        cost_estimate=cost(15, channels),
    )(forward_base, prior, gated, second_gate)
    carried, slab_all = lax.optimization_barrier((carried, slab_all))
    carried_all = swapped(carried.reshape(ctx, slab_width, tokens))

    length = ctx * tokens
    filter_rows = slab_all[:, slab_width:].transpose(1, 0, 2).reshape(own, 1, length).astype(wide)
    row_block = pl.BlockSpec((1, 1, length), lambda g: (g, 0, 0))
    piece = pl.BlockSpec((ctx, size, tokens), lambda g: (0, g, 0))
    all_shape = (ctx, slab_width, tokens)
    scratch = [
        pltpu.VMEM((tokens, length), narrow),
        pltpu.VMEM((ctx * size, 2 * tokens), narrow),
        pltpu.VMEM((ctx * size, tokens), wide),
    ]
    back_all = pl.pallas_call(
        back_kernel,
        grid=(own,),
        in_specs=[row_block, piece],
        out_specs=piece,
        out_shape=shape_of(all_shape, narrow),
        scratch_shapes=scratch,
        compiler_params=params,
        cost_estimate=cost(10, channels),
    )(filter_rows, slab_all)
    back_all, carried_all = lax.optimization_barrier((back_all, carried_all))
    back = swapped(back_all).reshape(channel_shape)

    scale = 1.0 / math.sqrt(length * size)
    ahead_all, long_rows = pl.pallas_call(
        functools.partial(ahead_kernel, scale),
        grid=(own,),
        in_specs=[row_block, piece, piece],
        out_specs=[piece, row_block],
        out_shape=[shape_of(all_shape, narrow), shape_of((own, 1, length), narrow)],
        scratch_shapes=scratch
        + [
            pltpu.VMEM((2 * ctx * size, tokens), narrow),
            pltpu.VMEM((tokens, length), wide),
        ],
        compiler_params=params,
        cost_estimate=cost(23, channels),
    )(filter_rows, carried_all, slab_all)
    ahead_all, long_rows, back = lax.optimization_barrier((ahead_all, long_rows, back))
    ahead = swapped(ahead_all).reshape(channel_shape)

    grad_second, grad_mixed, sums = pl.pallas_call(
        functools.partial(mixed_grad_kernel, size),
        grid=steps,
        in_specs=[by_channel, by_token, by_channel, by_channel, by_channel],
        out_specs=[by_token, by_channel, base_block],
        out_shape=[
            shape_of((tokens, channels), narrow),
            shape_of(channel_shape, narrow),
            shape_of((groups, 2 * tokens), wide),
        ],
        compiler_params=params,
        cost_estimate=cost(20, channels),
    )(back, second_gate, mixed, gated, prior)
    ahead, grad_mixed, sums = lax.optimization_barrier((ahead, grad_mixed, sums))
    after = lax.ppermute(grad_mixed, "ctx", [(i + 1, i) for i in range(ctx - 1)])

    terms = sums[:, tokens + 1 - taps : tokens + 1][:, ::-1] * scale
    long_pieces = long_rows.reshape(own, ctx, tokens).transpose(1, 0, 2).astype(wide)
    filter_terms = swapped(
        jnp.concatenate([terms.reshape(ctx, own, taps), long_pieces], axis=2)
    )
    grad_long = filter_terms[:, :, taps:].reshape(groups, tokens).T.astype(narrow)
    medium_own = jnp.sum(filter_terms[:, :, :taps], axis=0)
    squares = jnp.sum(jnp.square(medium_own)) + jnp.sum(jnp.square(long_rows.astype(wide)))
    package = jnp.concatenate([medium_own, jnp.full((1, taps), squares, wide)], axis=0)
    grad_output_gate = pl.pallas_call(
        output_grad_kernel,
        grid=steps,
        in_specs=[by_channel, by_token],
        out_specs=by_token,
        out_shape=shape_of((tokens, channels), narrow),
        compiler_params=params,
        cost_estimate=cost(6, channels),
    )(ahead, cotangent)
    package, after, grad_output_gate = lax.optimization_barrier(
        (package, after, grad_output_gate)
    )
    ch = lax.axis_size("ch")
    gathered = lax.all_to_all(
        jnp.broadcast_to(package[None], (ctx * ch, own + 1, taps)),
        ("ctx", "ch"),
        split_axis=0,
        concat_axis=0,
        tiled=True,
    ).reshape(ctx, ch, own + 1, taps)
    mine = lax.dynamic_index_in_dim(gathered, lax.axis_index("ch"), 1, keepdims=False)
    grad_medium = mine[:, :own].reshape(groups, taps).T
    total = jnp.sum(gathered[:, :, own, 0])
    filter_rms = jnp.sqrt(total / ((length + taps) * groups * ch))

    grad_first, grad_values = pl.pallas_call(
        functools.partial(gate_grad_kernel, size),
        grid=steps,
        in_specs=[base_block, by_channel, by_channel, by_token, by_token],
        out_specs=[by_token] * 2,
        out_shape=[shape_of((tokens, channels), narrow)] * 2,
        scratch_shapes=[pltpu.VMEM((width, tokens), wide)],
        compiler_params=params,
        cost_estimate=cost(15, channels),
    )(reverse_base, grad_mixed, after, first_gate, values)
    return (
        grad_first,
        grad_second,
        grad_output_gate,
        grad_values,
        grad_medium,
        grad_long,
        filter_rms,
    )


def solution(mesh):
    spread = P("ctx", "ch")
    shared = P(None, "ch")
    return jax.shard_map(
        body,
        mesh=mesh,
        in_specs=(spread, spread, spread, spread, spread, shared, spread),
        out_specs=(spread, spread, spread, spread, shared, spread, P()),
        check_vma=False,
    )
```

```python
import functools
import math

import jax
import jax.numpy as jnp
from jax import lax
from jax.experimental import pallas as pl
from jax.experimental.pallas import tpu as pltpu
from jax.sharding import PartitionSpec as P

wide = jnp.float32
narrow = jnp.bfloat16
params = pltpu.CompilerParams(vmem_limit_bytes=48 * 1024 * 1024)
peak = 1.1e9


def cost(micros, channels):
    scaled = int(micros * peak * channels / 4096)
    return pl.CostEstimate(flops=scaled, bytes_accessed=0, transcendentals=0)


def rolled_rows(row, rows):
    width = row.shape[1]
    base = pltpu.roll(jnp.broadcast_to(row, (16, width)), 0, 1, stride=1, stride_axis=0)
    base = base.astype(narrow)
    parts = [base]
    for number in range(1, rows // 16):
        parts.append(pltpu.roll(base, 16 * number, 1))
    return jnp.concatenate([part.astype(narrow) for part in parts], axis=0)


def diagonal_sums(table):
    rows, width = table.shape
    while rows > 8:
        rows = rows // 2
        table = table[:rows] + pltpu.roll(table[rows:], width - rows, 1)
    total = table[0:1]
    for number in range(1, rows):
        total = total + pltpu.roll(table[number : number + 1], width - number, 1)
    return total


def lower_mask(tokens):
    rows = lax.broadcasted_iota(jnp.int32, (tokens, tokens), 0)
    lanes = lax.broadcasted_iota(jnp.int32, (tokens, tokens), 1)
    return rows, lanes


def gated_kernel(first_ref, values_ref, gated_ref):
    gated = first_ref[...].astype(wide) * values_ref[...].astype(wide)
    gated_ref[...] = gated.astype(narrow).T


def inner_kernel(cotangent_ref, output_ref, filter_ref, slab_ref):
    inner = cotangent_ref[...].astype(wide) * output_ref[...].astype(wide)
    width = inner.shape[1]
    slab_ref[0, :width] = inner.astype(narrow).T
    slab_ref[0, width:] = filter_ref[0]


def forward_kernel(size, base_ref, prior_ref, gated_ref, second_ref, mixed_ref, carried_ref):
    gate = second_ref[...].T
    tokens = gated_ref.shape[1]
    row_ids, lane_ids = lower_mask(tokens)
    keep = jnp.where(lane_ids <= row_ids, 1.0, 0.0).astype(narrow)
    for number in range(base_ref.shape[0]):
        rows = slice(number * size, (number + 1) * size)
        extended = jnp.concatenate([prior_ref[rows], gated_ref[rows]], axis=1)
        whole = rolled_rows(base_ref[number : number + 1, :], tokens)
        near = whole * keep
        band = jnp.concatenate([whole - near, near], axis=1)
        mixed = lax.dot_general(
            extended, band, (((1,), (1,)), ((), ())), preferred_element_type=wide
        )
        mixed_ref[rows] = mixed
        carried_ref[rows] = (gate[rows].astype(wide) * mixed).astype(narrow)


def filter_table(row, block):
    table = rolled_rows(row, block)
    lanes = lax.broadcasted_iota(jnp.int32, (block, block), 1)
    rows = lax.broadcasted_iota(jnp.int32, (block, block), 0)
    head = jnp.where(lanes >= rows, table[:, :block].astype(wide), 0.0).astype(narrow)
    return head, table


def back_kernel(filter_ref, inner_ref, out_ref, table_ref, pair_ref, total_ref):
    blocks, size, block = inner_ref.shape
    count = blocks * size
    head, table = filter_table(filter_ref[0], block)
    table_ref[...] = table
    table_ref[:, :block] = head
    inner = inner_ref[...].reshape(count, block)
    pair_ref[:, :block] = inner
    pair_ref[: count - size, block:] = inner[size:]
    pair_ref[count - size :, block:] = jnp.zeros((size, block), narrow)
    for lag in range(0, blocks, 2):
        rows = count - lag * size
        product = lax.dot_general(
            pair_ref[lag * size :, :],
            table_ref[:, lag * block : (lag + 2) * block],
            (((1,), (1,)), ((), ())),
            preferred_element_type=wide,
        )
        if lag == 0:
            total_ref[...] = product
        else:
            total_ref[:rows] += product
    out_ref[...] = total_ref[...].astype(narrow).reshape(blocks, size, block)


def ahead_kernel(
    scale,
    filter_ref,
    carried_ref,
    inner_ref,
    out_ref,
    long_ref,
    table_ref,
    pair_ref,
    total_ref,
    padded_ref,
    lagged_ref,
):
    blocks, size, block = inner_ref.shape
    count = blocks * size
    head, table = filter_table(filter_ref[0], block)
    table_ref[...] = table
    table_ref[:, :block] = head
    carried = carried_ref[...].reshape(count, block)
    pair_ref[:, :block] = carried
    pair_ref[size:, block:] = carried[: count - size]
    pair_ref[:size, block:] = jnp.zeros((size, block), narrow)
    padded_ref[:count] = inner_ref[...].reshape(count, block)
    padded_ref[count:] = jnp.zeros((count, block), narrow)
    for lag in range(0, blocks, 2):
        rows = count - lag * size
        weights = jnp.concatenate(
            [
                table_ref[:, lag * block : (lag + 1) * block],
                table_ref[:, (lag + 1) * block : (lag + 2) * block],
            ],
            axis=0,
        )
        product = jnp.dot(pair_ref[:rows, :], weights, preferred_element_type=wide)
        if lag == 0:
            total_ref[...] = product
        else:
            total_ref[lag * size :] += product
    out_ref[...] = total_ref[...].astype(narrow).reshape(blocks, size, block)
    turned = carried.T
    for lag in range(0, blocks, 2):
        weights = jnp.concatenate(
            [
                padded_ref[lag * size : lag * size + count],
                padded_ref[(lag + 1) * size : (lag + 1) * size + count],
            ],
            axis=1,
        )
        lagged_ref[:, lag * block : (lag + 2) * block] = jnp.dot(
            turned, weights, preferred_element_type=wide
        )
    lanes = lax.broadcasted_iota(jnp.int32, (block, block), 1)
    rows = lax.broadcasted_iota(jnp.int32, (block, block), 0)
    lagged_ref[:, :block] = jnp.where(lanes >= rows, lagged_ref[:, :block], 0.0)
    long_ref[0] = (diagonal_sums(lagged_ref[...]) * scale).astype(narrow)


def mixed_grad_kernel(back_ref, second_ref, mixed_ref, grad_second_ref, grad_mixed_ref, token_ref):
    back = back_ref[...].astype(wide)
    grad_second_ref[...] = (back * mixed_ref[...]).T.astype(narrow)
    grad_mixed = (back_ref[...].T.astype(wide) * second_ref[...].astype(wide)).astype(narrow)
    token_ref[...] = grad_mixed
    grad_mixed_ref[...] = grad_mixed.T


def medium_kernel(size, grad_mixed_ref, gated_ref, prior_ref, sums_ref):
    tokens = grad_mixed_ref.shape[0]
    row_ids, lane_ids = lower_mask(tokens)
    keep = lane_ids <= row_ids
    grad_mixed = grad_mixed_ref[...]
    per = 128 // size
    for number in range(sums_ref.shape[0]):
        rows = slice(number * size, (number + 1) * size)
        extended = jnp.concatenate([prior_ref[rows], gated_ref[rows]], axis=1)
        place = number % per
        pieces = []
        if place > 0:
            pieces.append(jnp.zeros((place * size, 2 * tokens), narrow))
        pieces.append(extended)
        if place < per - 1:
            pieces.append(jnp.zeros(((per - 1 - place) * size, 2 * tokens), narrow))
        weights = jnp.concatenate(pieces, axis=0)
        start = number // per * 128
        product = jnp.dot(
            grad_mixed[:, start : start + 128], weights, preferred_element_type=wide
        )
        folded = jnp.where(keep, product[:, tokens:], product[:, :tokens])
        sums_ref[number : number + 1, :] = diagonal_sums(folded)


def gate_grad_kernel(
    size, base_ref, grad_mixed_ref, after_ref, first_ref, values_ref, grad_first_ref, grad_values_ref, total_ref
):
    tokens = grad_mixed_ref.shape[1]
    row_ids, lane_ids = lower_mask(tokens)
    keep = jnp.where(lane_ids >= row_ids, 1.0, 0.0).astype(narrow)
    for number in range(base_ref.shape[0]):
        rows = slice(number * size, (number + 1) * size)
        extended = jnp.concatenate([grad_mixed_ref[rows], after_ref[rows]], axis=1)
        whole = rolled_rows(base_ref[number : number + 1, :], tokens)
        near = whole * keep
        band = jnp.concatenate([near, whole - near], axis=1)
        total_ref[rows] = lax.dot_general(
            extended, band, (((1,), (1,)), ((), ())), preferred_element_type=wide
        )
    grad_gated = total_ref[...].T
    grad_first_ref[...] = (grad_gated * values_ref[...].astype(wide)).astype(narrow)
    grad_values_ref[...] = (grad_gated * first_ref[...].astype(wide)).astype(narrow)


def output_grad_kernel(ahead_ref, cotangent_ref, grad_output_ref):
    ahead = ahead_ref[...].T.astype(wide)
    grad_output_ref[...] = (cotangent_ref[...].astype(wide) * ahead).astype(narrow)


def shape_of(shape, kind):
    return jax.ShapeDtypeStruct(shape, kind)


def body(first_gate, second_gate, output_gate, values, cotangent, medium_filter, long_filter):
    tokens, channels = first_gate.shape
    taps, groups = medium_filter.shape
    size = channels // groups
    ctx = lax.axis_size("ctx")
    own = groups // ctx
    step_groups = math.gcd(groups, 16)
    width = step_groups * size
    steps = (groups // step_groups,)

    by_token = pl.BlockSpec((tokens, width), lambda i: (0, i))
    by_channel = pl.BlockSpec((width, tokens), lambda i: (i, 0))
    base_block = pl.BlockSpec((step_groups, tokens), lambda i: (i, 0))
    channel_shape = (channels, tokens)

    gated = pl.pallas_call(
        gated_kernel,
        grid=steps,
        in_specs=[by_token] * 2,
        out_specs=by_channel,
        out_shape=shape_of(channel_shape, narrow),
        compiler_params=params,
        cost_estimate=cost(5, channels),
    )(first_gate, values)
    prior = lax.ppermute(gated, "ctx", [(i, i + 1) for i in range(ctx - 1)])

    def swapped(array):
        return lax.all_to_all(array, "ctx", split_axis=0, concat_axis=0, tiled=True)

    slab_width = own * size
    slab_token = pl.BlockSpec((tokens, slab_width), lambda i: (0, i))
    if slab_width % 128:
        slab = jnp.concatenate(
            [
                (cotangent.astype(wide) * output_gate.astype(wide))
                .astype(narrow)
                .T.reshape(ctx, slab_width, tokens),
                long_filter.T.reshape(ctx, own, tokens),
            ],
            axis=1,
        )
    else:
        slab = pl.pallas_call(
            inner_kernel,
            grid=(ctx,),
            in_specs=[
                slab_token,
                slab_token,
                pl.BlockSpec((1, own, tokens), lambda i: (i, 0, 0)),
            ],
            out_specs=pl.BlockSpec((1, slab_width + own, tokens), lambda i: (i, 0, 0)),
            out_shape=shape_of((ctx, slab_width + own, tokens), narrow),
            compiler_params=params,
            cost_estimate=cost(5, channels),
        )(cotangent, output_gate, long_filter.T.reshape(ctx, own, tokens))
    slab_all = swapped(slab)

    turned = medium_filter.T.astype(wide)
    reverse_base = jnp.concatenate([turned, jnp.zeros((groups, tokens - taps), wide)], axis=1)
    forward_base = jnp.concatenate([reverse_base[:, :1], reverse_base[:, :0:-1]], axis=1)

    mixed, carried = pl.pallas_call(
        functools.partial(forward_kernel, size),
        grid=steps,
        in_specs=[base_block, by_channel, by_channel, by_token],
        out_specs=[by_channel] * 2,
        out_shape=[shape_of(channel_shape, wide), shape_of(channel_shape, narrow)],
        compiler_params=params,
        cost_estimate=cost(15, channels),
    )(forward_base, prior, gated, second_gate)
    carried_all = swapped(carried.reshape(ctx, slab_width, tokens))
    carried, slab_all = lax.optimization_barrier((carried, slab_all))

    length = ctx * tokens
    filter_rows = slab_all[:, slab_width:].transpose(1, 0, 2).reshape(own, 1, length).astype(wide)
    row_block = pl.BlockSpec((1, 1, length), lambda g: (g, 0, 0))
    piece = pl.BlockSpec((ctx, size, tokens), lambda g: (0, g, 0))
    all_shape = (ctx, slab_width, tokens)
    scratch = [
        pltpu.VMEM((tokens, length), narrow),
        pltpu.VMEM((ctx * size, 2 * tokens), narrow),
        pltpu.VMEM((ctx * size, tokens), wide),
    ]
    back_all = pl.pallas_call(
        back_kernel,
        grid=(own,),
        in_specs=[row_block, piece],
        out_specs=piece,
        out_shape=shape_of(all_shape, narrow),
        scratch_shapes=scratch,
        compiler_params=params,
        cost_estimate=cost(10, channels),
    )(filter_rows, slab_all)
    back_all, carried_all = lax.optimization_barrier((back_all, carried_all))
    back = swapped(back_all).reshape(channel_shape)

    scale = 1.0 / math.sqrt(length * size)
    ahead_all, long_rows = pl.pallas_call(
        functools.partial(ahead_kernel, scale),
        grid=(own,),
        in_specs=[row_block, piece, piece],
        out_specs=[piece, row_block],
        out_shape=[shape_of(all_shape, narrow), shape_of((own, 1, length), narrow)],
        scratch_shapes=scratch
        + [
            pltpu.VMEM((2 * ctx * size, tokens), narrow),
            pltpu.VMEM((tokens, length), wide),
        ],
        compiler_params=params,
        cost_estimate=cost(23, channels),
    )(filter_rows, carried_all, slab_all)
    ahead_all, long_rows, back = lax.optimization_barrier((ahead_all, long_rows, back))
    grad_second, grad_mixed, grad_token = pl.pallas_call(
        mixed_grad_kernel,
        grid=steps,
        in_specs=[by_channel, by_token, by_channel],
        out_specs=[by_token, by_channel, by_token],
        out_shape=[
            shape_of((tokens, channels), narrow),
            shape_of(channel_shape, narrow),
            shape_of((tokens, channels), narrow),
        ],
        compiler_params=params,
        cost_estimate=cost(7, channels),
    )(back, second_gate, mixed)
    after = lax.ppermute(grad_mixed, "ctx", [(i + 1, i) for i in range(ctx - 1)])
    ahead_all, grad_token = lax.optimization_barrier((ahead_all, grad_token))
    ahead = swapped(ahead_all).reshape(channel_shape)
    sums = pl.pallas_call(
        functools.partial(medium_kernel, size),
        grid=steps,
        in_specs=[by_token, by_channel, by_channel],
        out_specs=base_block,
        out_shape=shape_of((groups, tokens), wide),
        compiler_params=params,
        cost_estimate=cost(14, channels),
    )(grad_token, gated, prior)

    folded = jnp.concatenate([sums[:, :1], sums[:, :0:-1]], axis=1)
    folded, ahead = lax.optimization_barrier((folded, ahead))
    terms = folded[:, :taps] * scale
    long_pieces = long_rows.reshape(own, ctx, tokens).transpose(1, 0, 2).astype(wide)
    filter_terms = swapped(
        jnp.concatenate([terms.reshape(ctx, own, taps), long_pieces], axis=2)
    )
    grad_long = filter_terms[:, :, taps:].reshape(groups, tokens).T.astype(narrow)
    medium_own = jnp.sum(filter_terms[:, :, :taps], axis=0)
    squares = jnp.sum(jnp.square(medium_own)) + jnp.sum(jnp.square(long_rows.astype(wide)))
    package = jnp.concatenate([medium_own, jnp.full((1, taps), squares, wide)], axis=0)
    grad_first, grad_values = pl.pallas_call(
        functools.partial(gate_grad_kernel, size),
        grid=steps,
        in_specs=[base_block, by_channel, by_channel, by_token, by_token],
        out_specs=[by_token] * 2,
        out_shape=[shape_of((tokens, channels), narrow)] * 2,
        scratch_shapes=[pltpu.VMEM((width, tokens), wide)],
        compiler_params=params,
        cost_estimate=cost(15, channels),
    )(reverse_base, grad_mixed, after, first_gate, values)
    package, grad_first, grad_values, ahead = lax.optimization_barrier(
        (package, grad_first, grad_values, ahead)
    )
    ch = lax.axis_size("ch")
    gathered = lax.all_to_all(
        jnp.broadcast_to(package[None], (ctx * ch, own + 1, taps)),
        ("ctx", "ch"),
        split_axis=0,
        concat_axis=0,
        tiled=True,
    ).reshape(ctx, ch, own + 1, taps)
    mine = lax.dynamic_index_in_dim(gathered, lax.axis_index("ch"), 1, keepdims=False)
    grad_medium = mine[:, :own].reshape(groups, taps).T
    total = jnp.sum(gathered[:, :, own, 0])
    filter_rms = jnp.sqrt(total / ((length + taps) * groups * ch))

    grad_output_gate = pl.pallas_call(
        output_grad_kernel,
        grid=steps,
        in_specs=[by_channel, by_token],
        out_specs=by_token,
        out_shape=shape_of((tokens, channels), narrow),
        compiler_params=params,
        cost_estimate=cost(6, channels),
    )(ahead, cotangent)
    return (
        grad_first,
        grad_second,
        grad_output_gate,
        grad_values,
        grad_medium,
        grad_long,
        filter_rms,
    )


def solution(mesh):
    spread = P("ctx", "ch")
    shared = P(None, "ch")
    return jax.shard_map(
        body,
        mesh=mesh,
        in_specs=(spread, spread, spread, spread, spread, shared, spread),
        out_specs=(spread, spread, spread, spread, shared, spread, P()),
        check_vma=False,
    )
```

```python
import functools
import math

import jax
import jax.numpy as jnp
from jax import lax
from jax.experimental import pallas as pl
from jax.experimental.pallas import tpu as pltpu
from jax.sharding import PartitionSpec as P

wide = jnp.float32
narrow = jnp.bfloat16
params = pltpu.CompilerParams(vmem_limit_bytes=48 * 1024 * 1024)
peak = 1.1e9


def cost(micros, channels):
    scaled = int(micros * peak * channels / 4096)
    return pl.CostEstimate(flops=scaled, bytes_accessed=0, transcendentals=0)


def rolled_rows(row, rows):
    width = row.shape[1]
    base = pltpu.roll(jnp.broadcast_to(row, (16, width)), 0, 1, stride=1, stride_axis=0)
    base = base.astype(narrow)
    parts = [base]
    for number in range(1, rows // 16):
        parts.append(pltpu.roll(base, 16 * number, 1))
    return jnp.concatenate([part.astype(narrow) for part in parts], axis=0)


def diagonal_sums(table):
    rows, width = table.shape
    while rows > 8:
        rows = rows // 2
        table = table[:rows] + pltpu.roll(table[rows:], width - rows, 1)
    total = table[0:1]
    for number in range(1, rows):
        total = total + pltpu.roll(table[number : number + 1], width - number, 1)
    return total


def lower_mask(tokens):
    rows = lax.broadcasted_iota(jnp.int32, (tokens, tokens), 0)
    lanes = lax.broadcasted_iota(jnp.int32, (tokens, tokens), 1)
    return rows, lanes


def gated_kernel(first_ref, values_ref, gated_ref):
    gated = first_ref[...].astype(wide) * values_ref[...].astype(wide)
    gated_ref[...] = gated.astype(narrow).T


def inner_kernel(cotangent_ref, output_ref, filter_ref, slab_ref):
    inner = cotangent_ref[...].astype(wide) * output_ref[...].astype(wide)
    width = inner.shape[1]
    slab_ref[0, :width] = inner.astype(narrow).T
    slab_ref[0, width:] = filter_ref[0]


def forward_kernel(size, base_ref, prior_ref, gated_ref, second_ref, mixed_ref, carried_ref):
    gate = second_ref[...].T
    tokens = gated_ref.shape[1]
    row_ids, lane_ids = lower_mask(tokens)
    keep = jnp.where(lane_ids <= row_ids, 1.0, 0.0).astype(narrow)
    for number in range(base_ref.shape[0]):
        rows = slice(number * size, (number + 1) * size)
        extended = jnp.concatenate([prior_ref[rows], gated_ref[rows]], axis=1)
        whole = rolled_rows(base_ref[number : number + 1, :], tokens)
        near = whole * keep
        band = jnp.concatenate([whole - near, near], axis=1)
        mixed = lax.dot_general(
            extended, band, (((1,), (1,)), ((), ())), preferred_element_type=wide
        )
        mixed_ref[rows] = mixed
        carried_ref[rows] = (gate[rows].astype(wide) * mixed).astype(narrow)


def filter_table(row, block):
    table = rolled_rows(row, block)
    lanes = lax.broadcasted_iota(jnp.int32, (block, block), 1)
    rows = lax.broadcasted_iota(jnp.int32, (block, block), 0)
    head = jnp.where(lanes >= rows, table[:, :block].astype(wide), 0.0).astype(narrow)
    return head, table


def back_kernel(filter_ref, inner_ref, out_ref, table_ref, pair_ref, total_ref):
    blocks, size, block = inner_ref.shape
    count = blocks * size
    head, table = filter_table(filter_ref[0], block)
    table_ref[...] = table
    table_ref[:, :block] = head
    inner = inner_ref[...].reshape(count, block)
    pair_ref[:, :block] = inner
    pair_ref[: count - size, block:] = inner[size:]
    pair_ref[count - size :, block:] = jnp.zeros((size, block), narrow)
    for lag in range(0, blocks, 2):
        rows = count - lag * size
        product = lax.dot_general(
            pair_ref[lag * size :, :],
            table_ref[:, lag * block : (lag + 2) * block],
            (((1,), (1,)), ((), ())),
            preferred_element_type=wide,
        )
        if lag == 0:
            total_ref[...] = product
        else:
            total_ref[:rows] += product
    out_ref[...] = total_ref[...].astype(narrow).reshape(blocks, size, block)


def ahead_kernel(
    scale,
    filter_ref,
    carried_ref,
    inner_ref,
    out_ref,
    long_ref,
    table_ref,
    pair_ref,
    total_ref,
    padded_ref,
    lagged_ref,
):
    blocks, size, block = inner_ref.shape
    count = blocks * size
    head, table = filter_table(filter_ref[0], block)
    table_ref[...] = table
    table_ref[:, :block] = head
    carried = carried_ref[...].reshape(count, block)
    pair_ref[:, :block] = carried
    pair_ref[size:, block:] = carried[: count - size]
    pair_ref[:size, block:] = jnp.zeros((size, block), narrow)
    padded_ref[:count] = inner_ref[...].reshape(count, block)
    padded_ref[count:] = jnp.zeros((count, block), narrow)
    for lag in range(0, blocks, 2):
        rows = count - lag * size
        weights = jnp.concatenate(
            [
                table_ref[:, lag * block : (lag + 1) * block],
                table_ref[:, (lag + 1) * block : (lag + 2) * block],
            ],
            axis=0,
        )
        product = jnp.dot(pair_ref[:rows, :], weights, preferred_element_type=wide)
        if lag == 0:
            total_ref[...] = product
        else:
            total_ref[lag * size :] += product
    out_ref[...] = total_ref[...].astype(narrow).reshape(blocks, size, block)
    turned = carried.T
    for lag in range(0, blocks, 2):
        weights = jnp.concatenate(
            [
                padded_ref[lag * size : lag * size + count],
                padded_ref[(lag + 1) * size : (lag + 1) * size + count],
            ],
            axis=1,
        )
        lagged_ref[:, lag * block : (lag + 2) * block] = jnp.dot(
            turned, weights, preferred_element_type=wide
        )
    lanes = lax.broadcasted_iota(jnp.int32, (block, block), 1)
    rows = lax.broadcasted_iota(jnp.int32, (block, block), 0)
    lagged_ref[:, :block] = jnp.where(lanes >= rows, lagged_ref[:, :block], 0.0)
    long_ref[0] = (diagonal_sums(lagged_ref[...]) * scale).astype(narrow)


def mixed_grad_kernel(back_ref, second_ref, mixed_ref, grad_second_ref, grad_mixed_ref, token_ref):
    back = back_ref[...].astype(wide)
    grad_second_ref[...] = (back * mixed_ref[...]).T.astype(narrow)
    grad_mixed = (back_ref[...].T.astype(wide) * second_ref[...].astype(wide)).astype(narrow)
    token_ref[...] = grad_mixed
    grad_mixed_ref[...] = grad_mixed.T


def medium_kernel(size, grad_mixed_ref, gated_ref, prior_ref, sums_ref):
    tokens = grad_mixed_ref.shape[0]
    row_ids, lane_ids = lower_mask(tokens)
    keep = lane_ids <= row_ids
    grad_mixed = grad_mixed_ref[...]
    per = 128 // size
    for number in range(sums_ref.shape[0]):
        rows = slice(number * size, (number + 1) * size)
        extended = jnp.concatenate([prior_ref[rows], gated_ref[rows]], axis=1)
        place = number % per
        pieces = []
        if place > 0:
            pieces.append(jnp.zeros((place * size, 2 * tokens), narrow))
        pieces.append(extended)
        if place < per - 1:
            pieces.append(jnp.zeros(((per - 1 - place) * size, 2 * tokens), narrow))
        weights = jnp.concatenate(pieces, axis=0)
        start = number // per * 128
        product = jnp.dot(
            grad_mixed[:, start : start + 128], weights, preferred_element_type=wide
        )
        folded = jnp.where(keep, product[:, tokens:], product[:, :tokens])
        sums_ref[number : number + 1, :] = diagonal_sums(folded)


def gate_grad_kernel(
    size, base_ref, grad_mixed_ref, after_ref, first_ref, values_ref, grad_first_ref, grad_values_ref, total_ref
):
    tokens = grad_mixed_ref.shape[1]
    row_ids, lane_ids = lower_mask(tokens)
    keep = jnp.where(lane_ids >= row_ids, 1.0, 0.0).astype(narrow)
    for number in range(base_ref.shape[0]):
        rows = slice(number * size, (number + 1) * size)
        extended = jnp.concatenate([grad_mixed_ref[rows], after_ref[rows]], axis=1)
        whole = rolled_rows(base_ref[number : number + 1, :], tokens)
        near = whole * keep
        band = jnp.concatenate([near, whole - near], axis=1)
        total_ref[rows] = lax.dot_general(
            extended, band, (((1,), (1,)), ((), ())), preferred_element_type=wide
        )
    grad_gated = total_ref[...].T
    grad_first_ref[...] = (grad_gated * values_ref[...].astype(wide)).astype(narrow)
    grad_values_ref[...] = (grad_gated * first_ref[...].astype(wide)).astype(narrow)


def output_grad_kernel(ahead_ref, cotangent_ref, grad_output_ref):
    ahead = ahead_ref[...].T.astype(wide)
    grad_output_ref[...] = (cotangent_ref[...].astype(wide) * ahead).astype(narrow)


def shape_of(shape, kind):
    return jax.ShapeDtypeStruct(shape, kind)


def body(first_gate, second_gate, output_gate, values, cotangent, medium_filter, long_filter):
    tokens, channels = first_gate.shape
    taps, groups = medium_filter.shape
    size = channels // groups
    ctx = lax.axis_size("ctx")
    own = groups // ctx
    step_groups = math.gcd(groups, 16)
    width = step_groups * size
    steps = (groups // step_groups,)

    by_token = pl.BlockSpec((tokens, width), lambda i: (0, i))
    by_channel = pl.BlockSpec((width, tokens), lambda i: (i, 0))
    base_block = pl.BlockSpec((step_groups, tokens), lambda i: (i, 0))
    channel_shape = (channels, tokens)

    gated = pl.pallas_call(
        gated_kernel,
        grid=steps,
        in_specs=[by_token] * 2,
        out_specs=by_channel,
        out_shape=shape_of(channel_shape, narrow),
        compiler_params=params,
        cost_estimate=cost(5, channels),
    )(first_gate, values)
    prior = lax.ppermute(gated, "ctx", [(i, i + 1) for i in range(ctx - 1)])

    def swapped(array):
        return lax.all_to_all(array, "ctx", split_axis=0, concat_axis=0, tiled=True)

    slab_width = own * size
    slab_token = pl.BlockSpec((tokens, slab_width), lambda i: (0, i))
    if slab_width % 128:
        slab = jnp.concatenate(
            [
                (cotangent.astype(wide) * output_gate.astype(wide))
                .astype(narrow)
                .T.reshape(ctx, slab_width, tokens),
                long_filter.T.reshape(ctx, own, tokens),
            ],
            axis=1,
        )
    else:
        slab = pl.pallas_call(
            inner_kernel,
            grid=(ctx,),
            in_specs=[
                slab_token,
                slab_token,
                pl.BlockSpec((1, own, tokens), lambda i: (i, 0, 0)),
            ],
            out_specs=pl.BlockSpec((1, slab_width + own, tokens), lambda i: (i, 0, 0)),
            out_shape=shape_of((ctx, slab_width + own, tokens), narrow),
            compiler_params=params,
            cost_estimate=cost(5, channels),
        )(cotangent, output_gate, long_filter.T.reshape(ctx, own, tokens))
    slab_all = swapped(slab)

    turned = medium_filter.T.astype(wide)
    reverse_base = jnp.concatenate([turned, jnp.zeros((groups, tokens - taps), wide)], axis=1)
    forward_base = jnp.concatenate([reverse_base[:, :1], reverse_base[:, :0:-1]], axis=1)

    mixed, carried = pl.pallas_call(
        functools.partial(forward_kernel, size),
        grid=steps,
        in_specs=[base_block, by_channel, by_channel, by_token],
        out_specs=[by_channel] * 2,
        out_shape=[shape_of(channel_shape, wide), shape_of(channel_shape, narrow)],
        compiler_params=params,
        cost_estimate=cost(15, channels),
    )(forward_base, prior, gated, second_gate)
    carried_all = swapped(carried.reshape(ctx, slab_width, tokens))
    carried, slab_all = lax.optimization_barrier((carried, slab_all))

    length = ctx * tokens
    filter_rows = slab_all[:, slab_width:].transpose(1, 0, 2).reshape(own, 1, length).astype(wide)
    row_block = pl.BlockSpec((1, 1, length), lambda g: (g, 0, 0))
    piece = pl.BlockSpec((ctx, size, tokens), lambda g: (0, g, 0))
    all_shape = (ctx, slab_width, tokens)
    scratch = [
        pltpu.VMEM((tokens, length), narrow),
        pltpu.VMEM((ctx * size, 2 * tokens), narrow),
        pltpu.VMEM((ctx * size, tokens), wide),
    ]
    back_all = pl.pallas_call(
        back_kernel,
        grid=(own,),
        in_specs=[row_block, piece],
        out_specs=piece,
        out_shape=shape_of(all_shape, narrow),
        scratch_shapes=scratch,
        compiler_params=params,
        cost_estimate=cost(10, channels),
    )(filter_rows, slab_all)
    back_all, carried_all = lax.optimization_barrier((back_all, carried_all))
    back = swapped(back_all).reshape(channel_shape)

    scale = 1.0 / math.sqrt(length * size)
    ahead_all, long_rows = pl.pallas_call(
        functools.partial(ahead_kernel, scale),
        grid=(own,),
        in_specs=[row_block, piece, piece],
        out_specs=[piece, row_block],
        out_shape=[shape_of(all_shape, narrow), shape_of((own, 1, length), narrow)],
        scratch_shapes=scratch
        + [
            pltpu.VMEM((2 * ctx * size, tokens), narrow),
            pltpu.VMEM((tokens, length), wide),
        ],
        compiler_params=params,
        cost_estimate=cost(23, channels),
    )(filter_rows, carried_all, slab_all)
    ahead_all, long_rows, back = lax.optimization_barrier((ahead_all, long_rows, back))
    grad_second, grad_mixed, grad_token = pl.pallas_call(
        mixed_grad_kernel,
        grid=steps,
        in_specs=[by_channel, by_token, by_channel],
        out_specs=[by_token, by_channel, by_token],
        out_shape=[
            shape_of((tokens, channels), narrow),
            shape_of(channel_shape, narrow),
            shape_of((tokens, channels), narrow),
        ],
        compiler_params=params,
        cost_estimate=cost(7, channels),
    )(back, second_gate, mixed)
    after = lax.ppermute(grad_mixed, "ctx", [(i + 1, i) for i in range(ctx - 1)])
    ahead_all, grad_token = lax.optimization_barrier((ahead_all, grad_token))
    ahead = swapped(ahead_all).reshape(channel_shape)
    sums = pl.pallas_call(
        functools.partial(medium_kernel, size),
        grid=steps,
        in_specs=[by_token, by_channel, by_channel],
        out_specs=base_block,
        out_shape=shape_of((groups, tokens), wide),
        compiler_params=params,
        cost_estimate=cost(14, channels),
    )(grad_token, gated, prior)

    folded = jnp.concatenate([sums[:, :1], sums[:, :0:-1]], axis=1)
    folded, ahead = lax.optimization_barrier((folded, ahead))
    terms = folded[:, :taps] * scale
    long_pieces = long_rows.reshape(own, ctx, tokens).transpose(1, 0, 2).astype(wide)
    filter_terms = swapped(
        jnp.concatenate([terms.reshape(ctx, own, taps), long_pieces], axis=2)
    )
    grad_long = filter_terms[:, :, taps:].reshape(groups, tokens).T.astype(narrow)
    medium_own = jnp.sum(filter_terms[:, :, :taps], axis=0)
    squares = jnp.sum(jnp.square(medium_own)) + jnp.sum(jnp.square(long_rows.astype(wide)))
    package = jnp.concatenate([medium_own, jnp.full((1, taps), squares, wide)], axis=0)
    grad_output_gate = pl.pallas_call(
        output_grad_kernel,
        grid=steps,
        in_specs=[by_channel, by_token],
        out_specs=by_token,
        out_shape=shape_of((tokens, channels), narrow),
        compiler_params=params,
        cost_estimate=cost(6, channels),
    )(ahead, cotangent)
    package, after, grad_output_gate = lax.optimization_barrier(
        (package, after, grad_output_gate)
    )
    ch = lax.axis_size("ch")
    gathered = lax.all_to_all(
        jnp.broadcast_to(package[None], (ctx * ch, own + 1, taps)),
        ("ctx", "ch"),
        split_axis=0,
        concat_axis=0,
        tiled=True,
    ).reshape(ctx, ch, own + 1, taps)
    mine = lax.dynamic_index_in_dim(gathered, lax.axis_index("ch"), 1, keepdims=False)
    grad_medium = mine[:, :own].reshape(groups, taps).T
    total = jnp.sum(gathered[:, :, own, 0])
    filter_rms = jnp.sqrt(total / ((length + taps) * groups * ch))

    grad_first, grad_values = pl.pallas_call(
        functools.partial(gate_grad_kernel, size),
        grid=steps,
        in_specs=[base_block, by_channel, by_channel, by_token, by_token],
        out_specs=[by_token] * 2,
        out_shape=[shape_of((tokens, channels), narrow)] * 2,
        scratch_shapes=[pltpu.VMEM((width, tokens), wide)],
        compiler_params=params,
        cost_estimate=cost(15, channels),
    )(reverse_base, grad_mixed, after, first_gate, values)
    return (
        grad_first,
        grad_second,
        grad_output_gate,
        grad_values,
        grad_medium,
        grad_long,
        filter_rms,
    )


def solution(mesh):
    spread = P("ctx", "ch")
    shared = P(None, "ch")
    return jax.shard_map(
        body,
        mesh=mesh,
        in_specs=(spread, spread, spread, spread, spread, shared, spread),
        out_specs=(spread, spread, spread, spread, shared, spread, P()),
        check_vma=False,
    )
```
